32 devices in a mesh: grp: 4 (over y, core), dev: 8 (over z, x).
Axes of the slice: x: 2, y: 2, z: 4, core: 2. Of those that a mesh axis runs over, the one named last changes fastest.
Arguments:
- panels: bfloat16 [32, 1536, 512], P(('grp', 'dev')), may hold values from -0.19921875 to 0.19921875
- panel_owner: int32 [4, 3], replicated, may hold values from 0 to 7, as said below
- interface_cols: bfloat16 [1536, 8192], P(None, ('grp', 'dev')), may hold values from -6 to 6
- border: bfloat16 [4096, 1536], P('grp', 'dev'), may hold values from -0.15625 to 0.15625
- block_rows: int32 [4, 8], replicated, may hold values from 0 to 15, as said below
- pattern: int32 [16, 16], P('grp', 'dev'), may hold values 0 or 1
- block_x: bfloat16 [2048, 256], P('dev'), may hold values from -0.125 to 0.125
Outputs:
- schur: bfloat16 [2048, 2048], P('grp', 'dev')
- product: float32 [2048, 256], P('grp')
The draws below stay inside these ranges and needn't reach their ends.
Inputs may be any that keep to these rules, and one draw needn't show every extreme that they name: `panel_owner`: in each row the values are distinct. `block_rows`: in each row the values are distinct; for each subdomain the block rows with the same value of block // 4 (their owner group) come exactly 2 at a time; in every draw some owner group receives 2 block rows from every subdomain.
All inputs are finite; a program needn't handle non-finite values. No bound on the sum of `pattern` on one device may be relied on, other than what follows from the above.
Results may differ from the reference program's by a relative error of at most 0.017.
Values may be sent and summed in bfloat16 or wider, within the bound.
A program may use at most 64 MiB of HBM per device.

```python
import jax
import jax.numpy as jnp
from jax import lax

N = 1536
PW = 512
BR = 1024
RB = 128
XC = 256
CAP = 2
GROUPS = 4
DEVS = 8
NPAN = 3
BLK_GRP = 8
NSEL = 4
M = 2048
MB = 16
BPO = 4
GCOLS = 8192
N_GRP = 4
N_DEV = 8


def draw_panel_owner(key, part):
    keys = jax.random.split(jax.random.fold_in(key, 11), GROUPS)
    perms = jax.vmap(lambda single: jax.random.permutation(single, DEVS))(keys)
    return perms[:, :NPAN].astype(jnp.int32)


def draw_block_rows(key, part):
    base = jax.random.fold_in(key, 23)
    favored = jax.random.randint(jax.random.fold_in(base, 1), (), 0, GROUPS)
    keys = jax.random.split(jax.random.fold_in(base, 2), GROUPS)

    def one_group(single):
        first, second, third = jax.random.split(single, 3)
        scores = jax.random.randint(first, (GROUPS,), 0, GROUPS)
        scores = scores + jnp.where(jnp.arange(GROUPS) == favored, 2 * GROUPS, 0)
        distinct = scores * GROUPS + jnp.arange(GROUPS)
        chosen = jnp.argsort(-distinct, stable=True)[:NSEL]
        inner_keys = jax.random.split(second, NSEL)
        locals_ = jax.vmap(lambda sub: jax.random.permutation(sub, BPO)[:CAP])(inner_keys)
        blocks = (chosen[:, None] * BPO + locals_).reshape(-1)
        order = jax.random.permutation(third, BLK_GRP)
        return blocks[order]
    return jax.vmap(one_group)(keys).astype(jnp.int32)


def touch_ends(entries, key, smallest, largest):
    shape = entries.shape
    spot = [jax.random.randint(jax.random.fold_in(key, axis), (), 0, shape[axis]) for axis in range(len(shape))]
    entries = entries.at[tuple(spot)].set(smallest)
    longest = shape.index(max(shape))
    spot[longest] = (spot[longest] + 1) % shape[longest]
    return entries.at[tuple(spot)].set(largest)


def shard_levels(own_key, shape, cuts, low, high):
    level = 1.0
    for dim, parts in cuts:
        heights = jax.random.uniform(jax.random.fold_in(jax.random.fold_in(own_key, 6), dim), (parts,), jnp.float32, low / len(cuts), high / len(cuts))
        level = level * jnp.repeat(jnp.exp(heights), shape[dim] // parts).reshape((-1,) + (1,) * (len(shape) - 1 - dim))
    return level


def normal_values(rng, dims, width, most, shards=(), kind=jnp.bfloat16):
    gain = shard_levels(rng, dims, shards, -0.22, 0.18) if shards else 1.0
    entries = jax.random.normal(rng, dims, jnp.float32) * width * gain
    return jnp.minimum(jnp.maximum(entries, -most), most).astype(kind)


def setup_inputs(seed: int = 0) -> dict:
    arg_keys = jax.random.split(jax.random.key(seed), 8)
    return {
        "panels": normal_values(arg_keys[0], (N_GRP * N_DEV, N, PW), 0.03, 0.19921875, ((0, 32),)),
        "panel_owner": draw_panel_owner(jax.random.fold_in(arg_keys[7], 71), 0),
        "interface_cols": normal_values(arg_keys[2], (N, GCOLS), 1.0, 6.0, ((1, 32),)),
        "border": normal_values(arg_keys[3], (N_GRP * BR, N), N ** -0.5, 0.15625, ((0, 4), (1, 8))),
        "block_rows": draw_block_rows(jax.random.fold_in(arg_keys[7], 71), 0),
        "pattern": touch_ends((jax.random.randint(arg_keys[5], (MB, MB), 0, 4) < 3).astype(jnp.int32), jax.random.fold_in(arg_keys[5], 1), 0, 1),
        "block_x": normal_values(arg_keys[6], (M, XC), M ** -0.5, 0.125, ((0, 8),)),
    }


def solve_group(slots, owners, columns):
    lower = lax.broadcasted_iota(jnp.int32, (PW, PW), 0) > lax.broadcasted_iota(jnp.int32, (PW, PW), 1)
    unit = jnp.eye(PW, dtype=jnp.bfloat16)
    remain = [columns[step * PW:(step + 1) * PW].astype(jnp.float32) for step in range(NPAN)]
    solved = []
    for step in range(NPAN):
        slot = slots[owners[step]]
        diag_block = slot[step * PW:(step + 1) * PW]
        inverse = jnp.where(lower, diag_block, jnp.zeros((), jnp.bfloat16)) + unit
        current = jnp.dot(inverse, remain[step].astype(jnp.bfloat16), preferred_element_type=jnp.float32).astype(jnp.bfloat16)
        solved.append(current)
        if step + 1 < NPAN:
            below = jnp.dot(slot[(step + 1) * PW:], current, preferred_element_type=jnp.float32)
            for later in range(step + 1, NPAN):
                offset = (later - step - 1) * PW
                remain[later] = remain[later] - below[offset:offset + PW]
    return jnp.concatenate(solved, axis=0)


def reference(panels, panel_owner, interface_cols, border, block_rows, pattern, block_x):
    slots_all = panels.reshape(GROUPS, DEVS, N, PW)
    total = jnp.zeros((M, M), jnp.float32)
    inner = jnp.arange(RB, dtype=jnp.int32)
    for group in range(GROUPS):
        answer = solve_group(slots_all[group], panel_owner[group], interface_cols[:, group * M:(group + 1) * M])
        tile = jnp.dot(border[group * BR:(group + 1) * BR], answer, preferred_element_type=jnp.float32)
        targets = (block_rows[group][:, None] * RB + inner[None, :]).reshape(-1).astype(jnp.int32)
        total = total.at[targets].add(tile)
    masked = total.reshape(MB, RB, MB, RB) * pattern.astype(jnp.float32)[:, None, :, None]
    schur = masked.reshape(M, M).astype(jnp.bfloat16)
    product = jnp.dot(schur, block_x, preferred_element_type=jnp.float32)
    return schur, product
```

```python
import functools

import jax
import jax.numpy as jnp
from jax import lax
from jax.experimental import pallas as pl
from jax.experimental.pallas import tpu as pltpu
from jax.sharding import PartitionSpec as P

CAP = 2
ROWS = 128
SKEW = 1
MESH = pl.DeviceIdType.MESH


def columns_of(devs):
    side = 1
    for cand in range(1, devs + 1):
        if devs % cand == 0 and cand * cand <= devs:
            side = cand
    return side


def kernel(
    groups, devs, owner_ref, rows_ref, pat_ref, panel_ref, cols_ref, border_ref, x_ref,
    schur_ref, product_ref,
    packed, xrecv, right, left, full, bt, rt, yt, tile, out, inn, rs_out, rs_in, ag,
    xi_s, xi_r, r_s, r_r, l_s, l_r, f_s, f_r,
    br_s, br_r, bl_s, bl_r, ba_s, ba_r, bb_s, bb_r, g_s, g_r, rs_s, rs_r, ag_s, ag_r,
):
    B = columns_of(devs)
    A = devs // B
    me = lax.axis_index("dev")
    grp = lax.axis_index("grp")
    z = me // B
    x = me % B
    width = panel_ref.shape[2]
    height = panel_ref.shape[0] * ROWS
    npan = height // width
    cb = width // ROWS
    nslot = npan * cb
    per_slot = nslot // B
    lens = [(npan - k) * cb // B for k in range(npan)]
    base = [sum(lens[:k]) for k in range(npan + 1)]
    W = base[npan]
    ncols = cols_ref.shape[1]
    per_group = rows_ref.shape[1]
    owned = pat_ref.shape[0]
    col_blocks = pat_ref.shape[1]
    half = bt.shape[2]
    rb = tile.shape[2]
    piece = rs_out.shape[1]

    def copy(src, dst, ss, rs, **where):
        return pltpu.make_async_remote_copy(
            src_ref=src, dst_ref=dst, send_sem=ss, recv_sem=rs,
            device_id=where, device_id_type=MESH,
        )

    def xpeer(off):
        return z * B + (x + off) % B

    barrier = pltpu.get_barrier_semaphore()
    for off in range(1, devs):
        pl.semaphore_signal(barrier, inc=1, device_id={"dev": (me + off) % devs}, device_id_type=MESH)
    for off in range(1, groups):
        pl.semaphore_signal(barrier, inc=1, device_id={"grp": (grp + off) % groups}, device_id_type=MESH)

    kme = jnp.int32(0)
    for k in range(npan):
        kme = jnp.where(owner_ref[grp, k] == me, k, kme)
    for j in range(nslot):
        start = kme * cb + j
        packed[j] = panel_ref[jnp.where(start >= nslot, start - nslot, start)]
    for h in range(2):
        bt[me, h] = border_ref[h * half:(h + 1) * half, :]
    pl.semaphore_wait(barrier, devs + groups - 2)

    def xi(off, i):
        h = (x + off) % B
        return copy(packed.at[i * B + h], xrecv.at[B - off - 1, i], xi_s.at[off - 1, i],
                    xi_r.at[B - off - 1, i], dev=xpeer(off))

    def ba(off):
        return copy(bt.at[me, 0], bt.at[me, 0], ba_s.at[off - 1], ba_r.at[B - off - 1], dev=xpeer(off))

    def bb(off, o):
        ref = bt.at[o * B + x, 1]
        return copy(ref, ref, bb_s.at[off - 1, o], bb_r.at[B - off - 1, o], dev=xpeer(off))

    def fin(off, w):
        ref = full.at[w * B + x]
        return copy(ref, ref, f_s.at[off - 1, w], f_r.at[B - off - 1, w], dev=xpeer(off))

    def rsend(w):
        return copy(right.at[w], right.at[w], r_s.at[w], r_r.at[w], dev=(me + B) % devs)

    def lsend(w):
        return copy(left.at[w], left.at[w], l_s.at[w], l_r.at[w], dev=(me + devs - B) % devs)

    messages = [(1, 0)] + [(0, off) for off in range(B)]

    def brs(m, s):
        h, off = messages[m]
        ref = bt.at[(z - s) * B + (x + off) % B, h]
        return copy(ref, ref, br_s.at[m, s], br_r.at[m, s], dev=(me + B) % devs)

    def bls(m, s):
        h, off = messages[m]
        ref = bt.at[(z + s) * B + (x + off) % B, h]
        return copy(ref, ref, bl_s.at[m, s], bl_r.at[m, s], dev=(me + devs - B) % devs)

    def bwait(ref, sem):
        copy(ref, ref, sem, sem, dev=(me + 1) % devs).wait_recv()

    for i in range(per_slot):
        for off in range(1, B):
            xi(off, i).start()
        if i == 0:
            for off in range(1, B):
                ba(off).start()

    def border_hop(s):
        if s == 0:
            for off in range(1, B):
                bwait(bt.at[xpeer(off), 0], ba_r.at[off - 1])
            for off in range(1, B):
                bb(off, z).start()
        for m in range(len(messages)):
            h, off = messages[m]

            @pl.when(z - s >= 0)
            def _():
                o = z - s
                if s > 0:
                    bwait(bt.at[o * B + (x + off) % B, h], br_r.at[m, s - 1])
                    if h == 1:
                        for p in range(1, B):
                            bb(p, o).start()
                if s < A - 1:
                    @pl.when(z < A - 1)
                    def _():
                        brs(m, s).start()

            @pl.when(z + s <= A - 1)
            def _():
                o = z + s
                if s > 0:
                    bwait(bt.at[o * B + (x + off) % B, h], bl_r.at[m, s - 1])
                    if h == 1:
                        for p in range(1, B):
                            bb(p, o).start()
                if s < A - 1:
                    @pl.when(z > 0)
                    def _():
                        bls(m, s).start()

    def place(w):
        k = jnp.int32(0)
        first = jnp.int32(0)
        for kk in range(1, npan):
            k = jnp.where(w >= base[kk], kk, k)
            first = jnp.where(w >= base[kk], base[kk], first)
        own = owner_ref[grp, k]
        return own, w - first

    def value(own, i):
        v = packed[i * B + x]
        for off in range(1, B):
            v = jnp.where(own == xpeer(off), xrecv[off - 1, i], v)
        return v

    def step(t, _):
        @pl.when(t < per_slot)
        def _():
            for off in range(1, B):
                bwait(xrecv.at[off - 1, t], xi_r.at[off - 1, t])

        wr = t - SKEW * z
        @pl.when((wr >= 0) & (wr < W))
        def _():
            @pl.when(z > 0)
            def _():
                bwait(right.at[wr], r_r.at[wr])
            own, i = place(wr)
            right[wr] = jnp.where((own >= z * B) & (own < (z + 1) * B), value(own, i), right[wr])
            @pl.when(z < A - 1)
            def _():
                rsend(wr).start()

        wl = t - SKEW * (A - 1 - z)
        @pl.when((wl >= 0) & (wl < W))
        def _():
            @pl.when(z < A - 1)
            def _():
                bwait(left.at[wl], l_r.at[wl])
            own, i = place(wl)
            left[wl] = jnp.where((own >= z * B) & (own < (z + 1) * B), value(own, i), left[wl])
            @pl.when(z > 0)
            def _():
                lsend(wl).start()

        wf = t - SKEW * jnp.maximum(z, A - 1 - z)
        @pl.when((wf >= 0) & (wf < W))
        def _():
            own, _ = place(wf)
            full[wf * B + x] = jnp.where(own < (z + 1) * B, right[wf], left[wf])
            for off in range(1, B):
                fin(off, wf).start()
        return 0

    def run(t0, t1):
        lax.fori_loop(t0, t1, step, 0)

    last = W + SKEW * (A - 1)
    hops = {1 + (3 * s * per_slot) // 5: s for s in range(A)}
    marks = {min(base[k + 1] + SKEW * (A - 1) + 1, last): k for k in range(npan)}

    def solve(k):
        for w in range(base[k], base[k + 1]):
            for off in range(1, B):
                bwait(full.at[w * B + (x + off) % B], f_r.at[off - 1, w])
        first = base[k] * B
        lower = lax.broadcasted_iota(jnp.int32, (width, width), 0) > lax.broadcasted_iota(
            jnp.int32, (width, width), 1)
        diagonal = lax.broadcasted_iota(jnp.int32, (width, width), 0) == lax.broadcasted_iota(
            jnp.int32, (width, width), 1)
        block = full[first:first + cb].reshape(width, width).astype(jnp.float32)
        inverse = jnp.where(diagonal, 1.0, jnp.where(lower, block, 0.0)).astype(jnp.bfloat16)
        nt = (((1,), (1,)), ((), ()))
        current = lax.dot_general(
            rt[:, k * width:(k + 1) * width].astype(jnp.bfloat16), inverse, nt,
            preferred_element_type=jnp.float32).astype(jnp.bfloat16)
        yt[:, k * width:(k + 1) * width] = current
        for later in range(k + 1, npan):
            at = first + (later - k) * cb
            below = lax.dot_general(
                current, full[at:at + cb].reshape(width, width), nt,
                preferred_element_type=jnp.float32)
            rt[:, later * width:(later + 1) * width] -= below

    for k in range(npan):
        rt[:, k * width:(k + 1) * width] = jnp.transpose(
            cols_ref[k * width:(k + 1) * width, :].astype(jnp.float32))
    stops = sorted(set(hops) | set(marks) | {last})
    now = 0
    for stop in stops:
        if stop > now:
            run(now, min(stop, last))
            now = min(stop, last)
        if stop in hops:
            border_hop(hops[stop])
        if stop in marks:
            solve(marks[stop])

    for o in range(A):
        for off in range(1, B):
            bwait(bt.at[o * B + (x + off) % B, 1], bb_r.at[off - 1, o])
    answer = yt[...]
    for b in range(per_group // 2):
        both = bt[:, :, :, 2 * b * rb:2 * (b + 1) * rb].reshape(height, 2 * rb)
        got = jnp.dot(answer, both, preferred_element_type=jnp.float32)
        tile[2 * b] = got[:, :rb]
        tile[2 * b + 1] = got[:, rb:]

    def to_group(off):
        dst = (grp + off) % groups
        return copy(out.at[dst], inn.at[grp], g_s.at[off - 1], g_r.at[groups - off - 1], grp=dst)

    mine = [rows_ref[grp, b] for b in range(per_group)]
    for off in list(range(1, groups)) + [0]:
        dst = (grp + off) % groups
        for c in range(CAP):
            index, valid, seen = jnp.int32(0), jnp.int32(0), jnp.int32(0)
            for b in range(per_group):
                hit = (mine[b] >= dst * owned) & (mine[b] < (dst + 1) * owned)
                take = hit & (seen == c)
                index = jnp.where(take, b, index)
                valid = jnp.where(take, 1, valid)
                seen = jnp.where(hit, seen + 1, seen)
            block = jnp.where(valid == 1, tile[index], 0.0).astype(jnp.bfloat16)
            if off:
                out[dst, c] = block
            else:
                inn[grp, c] = block
        if off:
            to_group(off).start()
    for off in range(1, groups):
        src = (grp + off) % groups
        bwait(inn.at[src], g_r.at[off - 1])

    for j in range(owned):
        total = jnp.zeros((ncols, rb), jnp.float32)
        for s in range(groups):
            index, valid, seen = jnp.int32(0), jnp.int32(0), jnp.int32(0)
            for b in range(per_group):
                row = rows_ref[s, b]
                hit = (row >= grp * owned) & (row < (grp + 1) * owned)
                take = row == grp * owned + j
                index = jnp.where(take, jnp.minimum(seen, CAP - 1), index)
                valid = jnp.where(take, 1, valid)
                seen = jnp.where(hit, seen + 1, seen)
            total = total + jnp.where(valid == 1, inn[s, index].astype(jnp.float32), 0.0)
        parts = []
        for cbk in range(col_blocks):
            part = total[cbk * rb:(cbk + 1) * rb]
            parts.append(jnp.where(pat_ref[j, cbk] == 0, 0.0, part * pat_ref[j, cbk].astype(jnp.float32)))
        block = jnp.transpose(jnp.concatenate(parts, axis=0)).astype(jnp.bfloat16)
        schur_ref[j * rb:(j + 1) * rb, :] = block
        partial = jnp.dot(block, x_ref[...], preferred_element_type=jnp.float32).astype(jnp.bfloat16)
        per = rb // piece
        rs_out[j * per:(j + 1) * per] = partial.reshape(per, piece, partial.shape[1])

    def scatter(off):
        dst = (me + off) % devs
        return copy(rs_out.at[dst], rs_in.at[me], rs_s.at[off - 1], rs_r.at[devs - off - 1], dev=dst)

    def gather(off):
        dst = (me + off) % devs
        return copy(ag.at[me], ag.at[me], ag_s.at[off - 1], ag_r.at[devs - off - 1], dev=dst)

    for off in range(1, devs):
        scatter(off).start()
    total = rs_out[me].astype(jnp.float32)
    for off in range(1, devs):
        src = (me + off) % devs
        bwait(rs_in.at[src], rs_r.at[off - 1])
        total = total + rs_in[src].astype(jnp.float32)
    ag[me] = total.astype(jnp.bfloat16)
    for off in range(1, devs):
        gather(off).start()
    for off in range(1, devs):
        src = (me + off) % devs
        bwait(ag.at[src], ag_r.at[off - 1])
    product_ref[...] = ag[...].astype(jnp.float32).reshape(product_ref.shape)

    for off in range(1, B):
        ba(off).wait_send()
        for i in range(per_slot):
            xi(off, i).wait_send()
        for o in range(A):
            bb(off, o).wait_send()

    def drain(w, _):
        @pl.when(z < A - 1)
        def _():
            rsend(w).wait_send()
        @pl.when(z > 0)
        def _():
            lsend(w).wait_send()
        for off in range(1, B):
            fin(off, w).wait_send()
        return 0

    lax.fori_loop(0, W, drain, 0)
    for m in range(len(messages)):
        for s in range(A - 1):
            @pl.when((z - s >= 0) & (z < A - 1))
            def _():
                brs(m, s).wait_send()
            @pl.when((z + s <= A - 1) & (z > 0))
            def _():
                bls(m, s).wait_send()
    for off in range(1, groups):
        to_group(off).wait_send()
    for off in range(1, devs):
        scatter(off).wait_send()
        gather(off).wait_send()


def local(groups, devs, panels, panel_owner, interface_cols, border, block_rows, pattern, block_x):
    B = columns_of(devs)
    A = devs // B
    _, height, width = panels.shape
    npan = height // width
    cb = width // ROWS
    nslot = npan * cb
    W = sum((npan - k) * cb // B for k in range(npan))
    ncols = interface_cols.shape[1]
    rows, depth = border.shape
    per_group = block_rows.shape[1]
    owned = pattern.shape[0]
    rb = rows // per_group
    xc = block_x.shape[1]
    piece = owned * rb // devs
    bf, f32 = jnp.bfloat16, jnp.float32
    dma = pltpu.SemaphoreType.DMA
    m = B + 1
    vmem = pl.BlockSpec(memory_space=pltpu.VMEM)
    smem = pl.BlockSpec(memory_space=pltpu.SMEM)
    return pl.pallas_call(
        functools.partial(kernel, groups, devs),
        out_shape=(
            jax.ShapeDtypeStruct((owned * rb, ncols), bf),
            jax.ShapeDtypeStruct((owned * rb, xc), f32),
        ),
        in_specs=[smem, smem, smem, vmem, vmem, vmem, vmem],
        out_specs=(vmem, vmem),
        scratch_shapes=[
            pltpu.VMEM((nslot, ROWS, width), bf),
            pltpu.VMEM((B - 1, nslot // B, ROWS, width), bf),
            pltpu.VMEM((W, ROWS, width), bf),
            pltpu.VMEM((W, ROWS, width), bf),
            pltpu.VMEM((W * B, ROWS, width), bf),
            pltpu.VMEM((devs, 2, depth // 2, rows), bf),
            pltpu.VMEM((ncols, height), f32),
            pltpu.VMEM((ncols, height), bf),
            pltpu.VMEM((per_group, ncols, rb), f32),
            pltpu.VMEM((groups, CAP, ncols, rb), bf),
            pltpu.VMEM((groups, CAP, ncols, rb), bf),
            pltpu.VMEM((devs, piece, xc), bf),
            pltpu.VMEM((devs, piece, xc), bf),
            pltpu.VMEM((devs, piece, xc), bf),
            dma((B - 1, nslot // B)), dma((B - 1, nslot // B)),
            dma((W,)), dma((W,)), dma((W,)), dma((W,)),
            dma((B - 1, W)), dma((B - 1, W)),
            dma((m, A - 1)), dma((m, A - 1)), dma((m, A - 1)), dma((m, A - 1)),
            dma((B - 1,)), dma((B - 1,)), dma((B - 1, A)), dma((B - 1, A)),
            dma((groups - 1,)), dma((groups - 1,)),
            dma((devs - 1,)), dma((devs - 1,)), dma((devs - 1,)), dma((devs - 1,)),
        ],
        compiler_params=pltpu.CompilerParams(
            collective_id=0, has_side_effects=True, vmem_limit_bytes=48 * 1024 * 1024
        ),
    )(panel_owner, block_rows, pattern, panels.reshape(nslot, ROWS, width), interface_cols, border.T, block_x)


def solution(mesh):
    return jax.shard_map(
        functools.partial(local, mesh.shape["grp"], mesh.shape["dev"]),
        mesh=mesh,
        in_specs=(
            P(("grp", "dev"), None, None),
            P(),
            P(None, ("grp", "dev")),
            P("grp", "dev"),
            P(),
            P("grp", "dev"),
            P("dev", None),
        ),
        out_specs=(P("grp", "dev"), P("grp", None)),
        check_vma=False,
    )
```

```python
import functools

import jax
import jax.numpy as jnp
from jax import lax
from jax.experimental import pallas as pl
from jax.experimental.pallas import tpu as pltpu
from jax.sharding import PartitionSpec as P

CAP = 2
PARTS = 2
STRAIGHT = 0
SKEW = 3
MESH = pl.DeviceIdType.MESH


def columns_of(devs):
    side = 1
    for cand in range(1, devs + 1):
        if devs % cand == 0 and cand * cand <= devs:
            side = cand
    return side


def kernel(
    groups, devs, owner_ref, rows_ref, pat_ref, panel_ref, cols_ref, border_ref, x_ref,
    schur_ref, product_ref,
    packed, xrecv, right, left, full, bt, rt, yt, tile, out, inn, rs_out, rs_in, ag,
    xi_s, xi_r, r_s, r_r, l_s, l_r, f_s, f_r,
    br_s, br_r, bl_s, bl_r, ba_s, ba_r, bb_s, bb_r, g_s, g_r, rs_s, rs_r, ag_s, ag_r,
):
    B = columns_of(devs)
    A = devs // B
    me = lax.axis_index("dev")
    grp = lax.axis_index("grp")
    z = me // B
    x = me % B
    width = panel_ref.shape[2]
    rows = panel_ref.shape[1]
    height = panel_ref.shape[0] * rows
    npan = height // width
    cb = width // rows
    nfold = cb // 4
    cd = nfold + cb // 2
    nslot = cd + (npan - 1) * cb
    per_slot = nslot // B
    lens = [(cd + (npan - 1 - k) * cb) // B for k in range(npan)]
    base = [sum(lens[:k]) for k in range(npan + 1)]
    W = base[npan]
    ncols = cols_ref.shape[1]
    per_group = rows_ref.shape[1]
    owned = pat_ref.shape[0]
    col_blocks = pat_ref.shape[1]
    half = bt.shape[2]
    rb = tile.shape[2]
    piece = rs_out.shape[1]

    def copy(src, dst, ss, rs, **where):
        return pltpu.make_async_remote_copy(
            src_ref=src, dst_ref=dst, send_sem=ss, recv_sem=rs,
            device_id=where, device_id_type=MESH,
        )

    def xpeer(off):
        return z * B + (x + off) % B

    barrier = pltpu.get_barrier_semaphore()
    for off in range(1, devs):
        pl.semaphore_signal(barrier, inc=1, device_id={"dev": (me + off) % devs}, device_id_type=MESH)
    for off in range(1, groups):
        pl.semaphore_signal(barrier, inc=1, device_id={"grp": (grp + off) % groups}, device_id_type=MESH)

    kme = jnp.int32(0)
    for k in range(npan):
        kme = jnp.where(owner_ref[grp, k] == me, k, kme)

    def stored(j):
        start = kme * cb + j
        return panel_ref[jnp.where(start >= npan * cb, start - npan * cb, start)]

    for j in range(nfold):
        packed[j] = jnp.concatenate(
            [stored(j)[:, :width // 2], stored(j + nfold)[:, :width // 2]], axis=1)
    for j in range(cb // 2, npan * cb):
        packed[nfold + j - cb // 2] = stored(j)
    for h in range(PARTS):
        bt[me, h] = border_ref[h * half:(h + 1) * half, :]
    pl.semaphore_wait(barrier, devs + groups - 2)

    def xi(off, i):
        h = (x + off) % B
        return copy(packed.at[i * B + h], xrecv.at[B - off - 1, i], xi_s.at[off - 1, i],
                    xi_r.at[B - off - 1, i], dev=xpeer(off))

    def ba(off, h):
        ref = bt.at[me, h]
        return copy(ref, ref, ba_s.at[off - 1, h], ba_r.at[B - off - 1, h], dev=xpeer(off))

    def bb(off, h, o):
        ref = bt.at[o * B + x, h]
        return copy(ref, ref, bb_s.at[off - 1, h, o], bb_r.at[B - off - 1, h, o], dev=xpeer(off))

    def fin(off, w):
        ref = full.at[w * B + x]
        return copy(ref, ref, f_s.at[off - 1, w], f_r.at[B - off - 1, w], dev=xpeer(off))

    def rsend(w):
        return copy(right.at[w], right.at[w], r_s.at[w], r_r.at[w], dev=(me + B) % devs)

    def lsend(w):
        return copy(left.at[w], left.at[w], l_s.at[w], l_r.at[w], dev=(me + devs - B) % devs)

    messages = [(h, 0) for h in range(PARTS)] + [(h, off) for h in range(STRAIGHT) for off in range(1, B)]

    def brs(m, s):
        h, off = messages[m]
        ref = bt.at[(z - s) * B + (x + off) % B, h]
        return copy(ref, ref, br_s.at[m, s], br_r.at[m, s], dev=(me + B) % devs)

    def bls(m, s):
        h, off = messages[m]
        ref = bt.at[(z + s) * B + (x + off) % B, h]
        return copy(ref, ref, bl_s.at[m, s], bl_r.at[m, s], dev=(me + devs - B) % devs)

    def bwait(ref, sem):
        copy(ref, ref, sem, sem, dev=(me + 1) % devs).wait_recv()

    for i in range(per_slot):
        for off in range(1, B):
            xi(off, i).start()
        if i == 0:
            for off in range(1, B):
                for h in range(STRAIGHT):
                    ba(off, h).start()

    def border_hop(s):
        if s == 0:
            for off in range(1, B):
                for h in range(STRAIGHT):
                    bwait(bt.at[xpeer(off), h], ba_r.at[off - 1, h])
                for h in range(STRAIGHT, PARTS):
                    bb(off, h, z).start()
        for m in range(len(messages)):
            h, off = messages[m]

            @pl.when(z - s >= 0)
            def _():
                o = z - s
                if s > 0:
                    bwait(bt.at[o * B + (x + off) % B, h], br_r.at[m, s - 1])
                    if h >= STRAIGHT:
                        for p in range(1, B):
                            bb(p, h, o).start()
                if s < A - 1:
                    @pl.when(z < A - 1)
                    def _():
                        brs(m, s).start()

            @pl.when(z + s <= A - 1)
            def _():
                o = z + s
                if s > 0:
                    bwait(bt.at[o * B + (x + off) % B, h], bl_r.at[m, s - 1])
                    if h >= STRAIGHT:
                        for p in range(1, B):
                            bb(p, h, o).start()
                if s < A - 1:
                    @pl.when(z > 0)
                    def _():
                        bls(m, s).start()

    def place(w):
        k = jnp.int32(0)
        first = jnp.int32(0)
        for kk in range(1, npan):
            k = jnp.where(w >= base[kk], kk, k)
            first = jnp.where(w >= base[kk], base[kk], first)
        own = owner_ref[grp, k]
        return own, w - first

    def value(own, i):
        v = packed[i * B + x]
        for off in range(1, B):
            v = jnp.where(own == xpeer(off), xrecv[off - 1, i], v)
        return v

    def step(t, _):
        @pl.when(t < per_slot)
        def _():
            for off in range(1, B):
                bwait(xrecv.at[off - 1, t], xi_r.at[off - 1, t])

        wr = t - SKEW * z
        @pl.when((wr >= 0) & (wr < W))
        def _():
            @pl.when(z > 0)
            def _():
                bwait(right.at[wr], r_r.at[wr])
            own, i = place(wr)
            right[wr] = jnp.where((own >= z * B) & (own < (z + 1) * B), value(own, i), right[wr])
            @pl.when(z < A - 1)
            def _():
                rsend(wr).start()

        wl = t - SKEW * (A - 1 - z)
        @pl.when((wl >= 0) & (wl < W))
        def _():
            @pl.when(z < A - 1)
            def _():
                bwait(left.at[wl], l_r.at[wl])
            own, i = place(wl)
            left[wl] = jnp.where((own >= z * B) & (own < (z + 1) * B), value(own, i), left[wl])
            @pl.when(z > 0)
            def _():
                lsend(wl).start()

        wf = t - SKEW * jnp.maximum(z, A - 1 - z)
        @pl.when((wf >= 0) & (wf < W))
        def _():
            own, _ = place(wf)
            full[wf * B + x] = jnp.where(own < (z + 1) * B, right[wf], left[wf])
            for off in range(1, B):
                fin(off, wf).start()
        return 0

    def run(t0, t1):
        lax.fori_loop(t0, t1, step, 0)

    last = W + SKEW * (A - 1)
    hops = {last - 12 + 3 * s: s for s in range(A)}
    marks = {min(base[k + 1] + SKEW * (A - 1) + 1, last): k for k in range(npan)}

    def solve(k):
        for w in range(base[k], base[k + 1]):
            for off in range(1, B):
                bwait(full.at[w * B + (x + off) % B], f_r.at[off - 1, w])
        first = base[k] * B
        lower = lax.broadcasted_iota(jnp.int32, (width, width), 0) > lax.broadcasted_iota(
            jnp.int32, (width, width), 1)
        diagonal = lax.broadcasted_iota(jnp.int32, (width, width), 0) == lax.broadcasted_iota(
            jnp.int32, (width, width), 1)
        upper = full[first:first + nfold].reshape(width // 4, width)
        upper = jnp.concatenate([upper[:, :width // 2], upper[:, width // 2:]], axis=0)
        upper = jnp.concatenate([upper, jnp.zeros_like(upper)], axis=1)
        under = full[first + nfold:first + cd].reshape(width // 2, width)
        block = jnp.concatenate([upper, under], axis=0).astype(jnp.float32)
        inverse = jnp.where(diagonal, 1.0, jnp.where(lower, block, 0.0)).astype(jnp.bfloat16)
        nt = (((1,), (1,)), ((), ()))
        current = lax.dot_general(
            rt[:, k * width:(k + 1) * width].astype(jnp.bfloat16), inverse, nt,
            preferred_element_type=jnp.float32).astype(jnp.bfloat16)
        yt[:, k * width:(k + 1) * width] = current
        for later in range(k + 1, npan):
            at = first + cd + (later - k - 1) * cb
            below = lax.dot_general(
                current, full[at:at + cb].reshape(width, width), nt,
                preferred_element_type=jnp.float32)
            rt[:, later * width:(later + 1) * width] -= below

    for k in range(npan):
        rt[:, k * width:(k + 1) * width] = jnp.transpose(
            cols_ref[k * width:(k + 1) * width, :].astype(jnp.float32))
    stops = sorted(set(hops) | set(marks) | {last})
    now = 0
    for stop in stops:
        if stop > now:
            run(now, min(stop, last))
            now = min(stop, last)
        if stop in hops:
            border_hop(hops[stop])
        if stop in marks:
            solve(marks[stop])

    for o in range(A):
        for off in range(1, B):
            for h in range(STRAIGHT, PARTS):
                bwait(bt.at[o * B + (x + off) % B, h], bb_r.at[off - 1, h, o])
    answer = yt[...]
    for b in range(per_group // 2):
        both = bt[:, :, :, 2 * b * rb:2 * (b + 1) * rb].reshape(height, 2 * rb)
        got = jnp.dot(answer, both, preferred_element_type=jnp.float32)
        tile[2 * b] = got[:, :rb]
        tile[2 * b + 1] = got[:, rb:]

    def to_group(off):
        dst = (grp + off) % groups
        return copy(out.at[dst], inn.at[grp], g_s.at[off - 1], g_r.at[groups - off - 1], grp=dst)

    mine = [rows_ref[grp, b] for b in range(per_group)]
    for off in list(range(1, groups)) + [0]:
        dst = (grp + off) % groups
        for c in range(CAP):
            index, valid, seen = jnp.int32(0), jnp.int32(0), jnp.int32(0)
            for b in range(per_group):
                hit = (mine[b] >= dst * owned) & (mine[b] < (dst + 1) * owned)
                take = hit & (seen == c)
                index = jnp.where(take, b, index)
                valid = jnp.where(take, 1, valid)
                seen = jnp.where(hit, seen + 1, seen)
            block = jnp.where(valid == 1, tile[index], 0.0).astype(jnp.bfloat16)
            if off:
                out[dst, c] = block
            else:
                inn[grp, c] = block
        if off:
            to_group(off).start()
    for off in range(1, groups):
        src = (grp + off) % groups
        bwait(inn.at[src], g_r.at[off - 1])

    def scatter(dst):
        return copy(rs_out.at[dst], rs_in.at[me], rs_s.at[dst], rs_r.at[me], dev=dst)

    for j in range(owned):
        total = jnp.zeros((ncols, rb), jnp.float32)
        for s in range(groups):
            index, valid, seen = jnp.int32(0), jnp.int32(0), jnp.int32(0)
            for b in range(per_group):
                row = rows_ref[s, b]
                hit = (row >= grp * owned) & (row < (grp + 1) * owned)
                take = row == grp * owned + j
                index = jnp.where(take, jnp.minimum(seen, CAP - 1), index)
                valid = jnp.where(take, 1, valid)
                seen = jnp.where(hit, seen + 1, seen)
            total = total + jnp.where(valid == 1, inn[s, index].astype(jnp.float32), 0.0)
        parts = []
        for cbk in range(col_blocks):
            part = total[cbk * rb:(cbk + 1) * rb]
            parts.append(jnp.where(pat_ref[j, cbk] == 0, 0.0, part * pat_ref[j, cbk].astype(jnp.float32)))
        block = jnp.transpose(jnp.concatenate(parts, axis=0)).astype(jnp.bfloat16)
        schur_ref[j * rb:(j + 1) * rb, :] = block
        partial = jnp.dot(block, x_ref[...], preferred_element_type=jnp.float32).astype(jnp.bfloat16)
        per = rb // piece
        rs_out[j * per:(j + 1) * per] = partial.reshape(per, piece, partial.shape[1])
        for dst in range(j * per, (j + 1) * per):
            @pl.when(dst != me)
            def _():
                scatter(dst).start()

    def gather(off):
        dst = (me + off) % devs
        return copy(ag.at[me], ag.at[me], ag_s.at[off - 1], ag_r.at[devs - off - 1], dev=dst)

    total = rs_out[me].astype(jnp.float32)
    for off in range(1, devs):
        src = (me + off) % devs
        bwait(rs_in.at[src], rs_r.at[src])
        total = total + rs_in[src].astype(jnp.float32)
    ag[me] = total.astype(jnp.bfloat16)
    for off in range(1, devs):
        gather(off).start()
    for off in range(1, devs):
        src = (me + off) % devs
        bwait(ag.at[src], ag_r.at[off - 1])
    product_ref[...] = ag[...].astype(jnp.float32).reshape(product_ref.shape)

    for off in range(1, B):
        for h in range(STRAIGHT):
            ba(off, h).wait_send()
        for i in range(per_slot):
            xi(off, i).wait_send()
        for o in range(A):
            for h in range(STRAIGHT, PARTS):
                bb(off, h, o).wait_send()

    def drain(w, _):
        @pl.when(z < A - 1)
        def _():
            rsend(w).wait_send()
        @pl.when(z > 0)
        def _():
            lsend(w).wait_send()
        for off in range(1, B):
            fin(off, w).wait_send()
        return 0

    lax.fori_loop(0, W, drain, 0)
    for m in range(len(messages)):
        for s in range(A - 1):
            @pl.when((z - s >= 0) & (z < A - 1))
            def _():
                brs(m, s).wait_send()
            @pl.when((z + s <= A - 1) & (z > 0))
            def _():
                bls(m, s).wait_send()
    for off in range(1, groups):
        to_group(off).wait_send()
    for off in range(1, devs):
        scatter((me + off) % devs).wait_send()
        gather(off).wait_send()


def local(groups, devs, panels, panel_owner, interface_cols, border, block_rows, pattern, block_x):
    B = columns_of(devs)
    A = devs // B
    _, height, width = panels.shape
    npan = height // width
    rows_of = width // (4 * B)
    cb = width // rows_of
    cd = 3 * cb // 4
    nslot = cd + (npan - 1) * cb
    W = sum((cd + (npan - 1 - k) * cb) // B for k in range(npan))
    ncols = interface_cols.shape[1]
    rows, depth = border.shape
    per_group = block_rows.shape[1]
    owned = pattern.shape[0]
    rb = rows // per_group
    xc = block_x.shape[1]
    piece = owned * rb // devs
    bf, f32 = jnp.bfloat16, jnp.float32
    dma = pltpu.SemaphoreType.DMA
    m = PARTS + STRAIGHT * (B - 1)
    vmem = pl.BlockSpec(memory_space=pltpu.VMEM)
    smem = pl.BlockSpec(memory_space=pltpu.SMEM)
    return pl.pallas_call(
        functools.partial(kernel, groups, devs),
        out_shape=(
            jax.ShapeDtypeStruct((owned * rb, ncols), bf),
            jax.ShapeDtypeStruct((owned * rb, xc), f32),
        ),
        in_specs=[smem, smem, smem, vmem, vmem, vmem, vmem],
        out_specs=(vmem, vmem),
        scratch_shapes=[
            pltpu.VMEM((nslot, rows_of, width), bf),
            pltpu.VMEM((B - 1, nslot // B, rows_of, width), bf),
            pltpu.VMEM((W, rows_of, width), bf),
            pltpu.VMEM((W, rows_of, width), bf),
            pltpu.VMEM((W * B, rows_of, width), bf),
            pltpu.VMEM((devs, PARTS, depth // PARTS, rows), bf),
            pltpu.VMEM((ncols, height), f32),
            pltpu.VMEM((ncols, height), bf),
            pltpu.VMEM((per_group, ncols, rb), f32),
            pltpu.VMEM((groups, CAP, ncols, rb), bf),
            pltpu.VMEM((groups, CAP, ncols, rb), bf),
            pltpu.VMEM((devs, piece, xc), bf),
            pltpu.VMEM((devs, piece, xc), bf),
            pltpu.VMEM((devs, piece, xc), bf),
            dma((B - 1, nslot // B)), dma((B - 1, nslot // B)),
            dma((W,)), dma((W,)), dma((W,)), dma((W,)),
            dma((B - 1, W)), dma((B - 1, W)),
            dma((m, A - 1)), dma((m, A - 1)), dma((m, A - 1)), dma((m, A - 1)),
            dma((B - 1, PARTS)), dma((B - 1, PARTS)), dma((B - 1, PARTS, A)), dma((B - 1, PARTS, A)),
            dma((groups - 1,)), dma((groups - 1,)),
            dma((devs,)), dma((devs,)), dma((devs - 1,)), dma((devs - 1,)),
        ],
        compiler_params=pltpu.CompilerParams(
            collective_id=0, has_side_effects=True, vmem_limit_bytes=48 * 1024 * 1024
        ),
    )(panel_owner, block_rows, pattern, panels.reshape(npan * cb, rows_of, width), interface_cols, border.T, block_x)


def solution(mesh):
    return jax.shard_map(
        functools.partial(local, mesh.shape["grp"], mesh.shape["dev"]),
        mesh=mesh,
        in_specs=(
            P(("grp", "dev"), None, None),
            P(),
            P(None, ("grp", "dev")),
            P("grp", "dev"),
            P(),
            P("grp", "dev"),
            P("dev", None),
        ),
        out_specs=(P("grp", "dev"), P("grp", None)),
        check_vma=False,
    )
```
